32 devices in a mesh: groups: 2 (over y), grid: 4 (over z), band: 2 (over x), sub: 2 (over core).
Axes of the slice: x: 2, y: 2, z: 4, core: 2. Of those that a mesh axis runs over, the one named last changes fastest.
Arguments:
- filter_block: float32 [4, 32, 16, 8, 128], P(('groups', 'band'), 'grid', 'sub'), parts along dimension 0, may hold values from -300 to 300
- band_blocks: float32 [4, 2, 32, 16, 8, 128], P(('groups', 'band'), None, 'grid', 'sub'), parts along dimension 0, may hold values from -6 to 6
- potential: float32 [64, 16, 8], P(('groups', 'grid'), 'sub'), parts along dimension 0, may hold values from -1 to 4
- atom_plane: int32 [4096], P('groups'), parts along dimension 0, may hold values from 0 to 31
- block_slot: int32 [8], P('groups'), parts along dimension 0, may hold values from 0 to 3, each once
Outputs:
- correlation: float32 [4, 4, 128, 128], P(('groups', 'band')), parts along dimension 0
- energy: float32 [4, 4, 128, 128], P(('groups', 'band')), parts along dimension 0
The draws below stay inside these ranges and needn't reach their ends.
There are 2 independent parts, one for each index of `groups`. The reference program is written for one: setup_inputs(seed, part) draws one part's arguments, and reference() takes and returns one part's arrays. A program takes and returns all parts, laid end to end along the dimension named above; each array names one. Nothing has to cross between parts.
All inputs are finite; a program needn't handle non-finite values.
Results may differ from the reference program's by a relative error of at most 0.0001.
Values sent between devices are 32-bit elements; how exact they have to be, the bound alone decides.
A program may use at most 64 MiB of HBM per device.

```python
import math
import jax
import jax.numpy as jnp
from jax import lax

BLOCK = 128
CX = 8
ATOMS = 2048
NZ = 32
NY = 16
N_BAND = 2


def draw_filter_block(key, part):
    key = jax.random.fold_in(key, 11)
    first_key, second_key = jax.random.split(key, 2)
    depth = (jnp.arange(NZ, dtype=jnp.float32) / NZ)[None, :, None, None, None]
    columns = jnp.exp(jax.random.uniform(second_key, (N_BAND, 1, 1, 1, BLOCK), jnp.float32, 0.0, math.log(10.0)))
    base = jnp.clip(jax.random.normal(first_key, (N_BAND, NZ, NY, CX, BLOCK), jnp.float32), -6.0, 6.0)
    ramp = 1.0 + 2.0 * depth
    return base * ramp * columns


def draw_potential(key, part):
    key = jax.random.fold_in(key, 7)
    depth = (jnp.arange(NZ, dtype=jnp.float32) / NZ)[:, None, None]
    rough = jax.random.uniform(key, (NZ, NY, CX), jnp.float32, -0.5, 0.5)
    return 3.0 * depth + rough


def with_ends(array, key, low, top_value):
    extent = array.shape
    place = [jax.random.randint(jax.random.fold_in(key, axis), (), 0, extent[axis]) for axis in range(len(extent))]
    array = array.at[tuple(place)].set(low)
    longest = extent.index(max(extent))
    place[longest] = (place[longest] + 1) % extent[longest]
    return array.at[tuple(place)].set(top_value)


def level_of(rng, dims, cuts, smallest, top_value):
    level, own = 1.0, jax.random.fold_in(rng, 6)
    for position, blocks in cuts:
        draws = jnp.exp(jax.random.uniform(jax.random.fold_in(own, position), (blocks,), jnp.float32, smallest / len(cuts), top_value / len(cuts)))
        level = level * jnp.repeat(draws, dims[position] // blocks).reshape([-1 if axis == position else 1 for axis in range(len(dims))])
    return level


def centred(key, shape, width, reach, pieces=(), held_as=jnp.bfloat16):
    entries = jax.random.normal(key, shape, jnp.float32) * width
    if len(pieces) > 0:
        entries = level_of(key, shape, pieces, -0.22, 0.18) * entries
    return jnp.clip(entries, min=-reach, max=reach).astype(held_as)


def setup_inputs(seed: int = 0, part: int = 0) -> dict:
    splits = jax.random.split(jax.random.key(seed), 6)
    own_keys = jax.random.split(jax.random.fold_in(splits[5], part), 6)
    return {
        "filter_block": draw_filter_block(jax.random.fold_in(jax.random.fold_in(splits[5], part), 71), part),
        "band_blocks": centred(own_keys[1], (N_BAND, 2, NZ, NY, CX, BLOCK), 1.0, 6.0, ((0, 2), (2, 4), (3, 2)), jnp.float32),
        "potential": draw_potential(jax.random.fold_in(jax.random.fold_in(splits[5], part), 71), part),
        "atom_plane": with_ends(jax.random.randint(own_keys[3], (ATOMS,), 0, NZ), jax.random.fold_in(own_keys[3], 1), 0, NZ - 1).astype(jnp.int32),
        "block_slot": jax.random.permutation(own_keys[4], 2 * N_BAND).astype(jnp.int32),
    }


STENCIL = (-205.0 / 72.0, 8.0 / 5.0, -1.0 / 5.0, 8.0 / 315.0, -1.0 / 560.0)
LOWER_EDGE = 1.0
KINETIC_TOP = 10.0
EPSILON = 1e-06

def hamiltonian(orbital, effective):
    summed = 3.0 * STENCIL[0] * orbital
    for shift_by in range(1, 5):
        beside_all = jnp.roll(orbital, shift_by, 0) + jnp.roll(orbital, -shift_by, 0)
        beside_all = beside_all + jnp.roll(orbital, shift_by, 1) + jnp.roll(orbital, -shift_by, 1)
        beside_all = beside_all + jnp.roll(orbital, shift_by, 2) + jnp.roll(orbital, -shift_by, 2)
        summed = summed + STENCIL[shift_by] * beside_all
    return -0.5 * summed + effective[:, :, :, None] * orbital

def reference(filter_block, band_blocks, potential, atom_plane, block_slot):
    planes = jnp.arange(NZ, dtype=jnp.int32)
    counts = lax.optimization_barrier(jnp.sum((planes[:, None] == atom_plane[None, :]).astype(jnp.float32), axis=1))
    effective = potential + (counts * (NZ / ATOMS))[:, None, None]
    ceiling = KINETIC_TOP + jnp.max(effective)
    centre = 0.5 * (ceiling + LOWER_EDGE)
    spread = 0.5 * (ceiling - LOWER_EDGE)
    cells_all = NZ * NY * CX
    stored = band_blocks.reshape(2 * N_BAND, cells_all, BLOCK)
    correlations = []
    energies = []
    for block_index in range(N_BAND):
        orbital = filter_block[block_index]
        section_one = (hamiltonian(orbital, effective) - centre * orbital) / spread
        section_two = 2.0 * (hamiltonian(section_one, effective) - centre * section_one) / spread - orbital
        applied = hamiltonian(section_two, effective)
        column_scale = lax.rsqrt(lax.optimization_barrier(jnp.sum(section_two * section_two, axis=(0, 1, 2))) / cells_all + EPSILON)
        both = jnp.concatenate((section_two.reshape(cells_all, BLOCK), applied.reshape(cells_all, BLOCK)), axis=1)
        products = jnp.einsum('kcb,cd->kbd', stored, both, precision=lax.Precision.HIGHEST)
        factor = jnp.concatenate((column_scale, column_scale)) / jnp.sqrt(jnp.float32(cells_all))
        products = products * factor[None, None, :]
        placed = jnp.zeros_like(products).at[block_slot].set(products)
        correlations.append(placed[:, :, :BLOCK])
        energies.append(placed[:, :, BLOCK:])
    return (jnp.stack(correlations), jnp.stack(energies))
```

```python
import functools
import math

import jax
import jax.numpy as jnp
from jax import lax
from jax.experimental import pallas as pl
from jax.experimental.pallas import tpu as pltpu
from jax.sharding import PartitionSpec as P

STENCIL = (-205.0 / 72.0, 8.0 / 5.0, -1.0 / 5.0, 8.0 / 315.0, -1.0 / 560.0)
LOWER_EDGE = 1.0
KINETIC_TOP = 10.0
EPSILON = 1e-06
HALO = 4
CHUNKS = 4
MESH = pl.DeviceIdType.MESH


def remote(src, dst, send_sem, recv_sem, **device):
    return pltpu.make_async_remote_copy(
        src_ref=src,
        dst_ref=dst,
        send_sem=send_sem,
        recv_sem=recv_sem,
        device_id=device,
        device_id_type=MESH,
    )


def split(value):
    high = value.astype(jnp.bfloat16)
    return high, (value - high.astype(jnp.float32)).astype(jnp.bfloat16)


def kernel(
    nz, nb, x_hbm, q_hbm, pot, atoms, out,
    f0, f1, f2, applied, acc, eff, ypeer, qbuf, qt_high, qt_low,
    consts, tops, squares, part_out, part_in, part_sum, from_low, from_high, to_high, to_low,
    load_sem, z_send, z_recv, y_send, y_recv, q_send, q_recv,
    top_send, top_recv, square_send, square_recv, part_send, part_recv,
    up_send, up_recv, down_send, down_recv, out_send, out_recv,
):
    g, s, b = lax.axis_index("grid"), lax.axis_index("sub"), lax.axis_index("band")
    other = 1 - s
    above, below = lax.rem(g + 1, nz), lax.rem(g + nz - 1, nz)
    depth_z, depth_y, width_x, orbitals = acc.shape
    ranks = 2 * nz
    me = 2 * g + s
    planes_all = nz * depth_z
    cells_dev = depth_z * depth_y * width_x
    cells_all = cells_dev * ranks
    half = nb * orbitals
    chunk = half // CHUNKS
    fields = (f0, f1, f2)
    lower_half = depth_z // 2

    loads = [pltpu.make_async_copy(x_hbm.at[0], f0.at[pl.ds(HALO, depth_z)], load_sem.at[0])]
    for slot in range(2):
        loads.append(
            pltpu.make_async_copy(q_hbm.at[0, slot], qbuf.at[2 * b + slot], load_sem.at[1 + slot])
        )
    for load in loads:
        load.start()

    barrier = pltpu.get_barrier_semaphore()

    def greet(step, carry):
        rank = lax.rem(me + step, ranks)
        pl.semaphore_signal(
            barrier, inc=1, device_id={"grid": rank // 2, "sub": lax.rem(rank, 2)}, device_id_type=MESH
        )
        return carry

    lax.fori_loop(1, ranks, greet, 0)
    for step in range(1, nb):
        pl.semaphore_signal(
            barrier, inc=1, device_id={"band": lax.rem(b + step, nb)}, device_id_type=MESH
        )
    pl.semaphore_wait(barrier, ranks - 1 + nb - 1)

    def z_copy(step, side):
        field = fields[step]
        if side == 0:
            src = pl.ds(HALO, HALO)
            dst = field.at[pl.ds(HALO + depth_z, HALO)]
            where = below
        else:
            src = pl.ds(depth_z, HALO)
            dst = field.at[pl.ds(0, HALO)]
            where = above
        source = field.at[src]
        if step == 0:
            source = x_hbm.at[0, pl.ds(0 if side == 0 else depth_z - HALO, HALO)]
        return remote(source, dst, z_send.at[step, side], z_recv.at[step, 1 - side], grid=where)

    def y_copy(step, side):
        planes = pl.ds(side * lower_half, lower_half)
        source = fields[step].at[pl.ds(HALO + side * lower_half, lower_half)]
        if step == 0:
            source = x_hbm.at[0, planes]
        return remote(
            source, ypeer.at[step, planes], y_send.at[step, side], y_recv.at[step, side], sub=other
        )

    def q_copy(step, slot):
        return remote(
            q_hbm.at[0, slot], qbuf.at[2 * b + slot],
            q_send.at[step - 1, slot], q_recv.at[step - 1, slot], band=lax.rem(b + step, nb),
        )

    for side in range(2):
        z_copy(0, side).start()
    for side in range(2):
        y_copy(0, side).start()
    for step in range(1, nb):
        for slot in range(2):
            q_copy(step, slot).start()

    centre_term = -0.5 * 3.0 * STENCIL[0]
    eye = lax.broadcasted_iota(jnp.int32, (width_x, width_x), 0) == lax.broadcasted_iota(
        jnp.int32, (width_x, width_x), 1
    )
    atom_total = atoms.shape[0] * atoms.shape[1]

    def plane_potential(p, top):
        hits = jnp.where(atoms[...] == g * depth_z + p, 1.0, 0.0)
        count = jnp.sum(jnp.sum(hits, axis=0, keepdims=True), axis=1, keepdims=True)
        offset = count * (planes_all / atom_total)
        for y in range(depth_y):
            row = jnp.broadcast_to(pot[p, pl.ds(y, 1), :], (width_x, width_x))
            column = jnp.sum(jnp.where(eye, row, 0.0), axis=1, keepdims=True)
            cell = jnp.broadcast_to(column + offset, (width_x, orbitals))
            top = jnp.maximum(top, cell)
            eff[p, y] = cell + centre_term
        return top

    tops[me] = lax.fori_loop(
        0, depth_z, plane_potential, jnp.full((width_x, orbitals), -jnp.inf, jnp.float32)
    )

    def rank_copy(buffer, send_sem, recv_sem, step):
        rank = lax.rem(me + step, ranks)
        return remote(
            buffer.at[me], buffer.at[me], send_sem.at[step], recv_sem.at[step],
            grid=rank // 2, sub=lax.rem(rank, 2),
        )

    def send_ranks(buffer, send_sem, recv_sem):
        def one(step, carry):
            rank_copy(buffer, send_sem, recv_sem, step).start()
            return carry

        lax.fori_loop(1, ranks, one, 0)

    def wait_ranks(buffer, send_sem, recv_sem):
        def one(step, carry):
            rank_copy(buffer, send_sem, recv_sem, step).wait_recv()
            return carry

        lax.fori_loop(1, ranks, one, 0)

    send_ranks(tops, top_send, top_recv)

    def pre(step):
        field = fields[step]
        for side in range(2):
            y_copy(step, side).wait_recv()

        def one(p, carry):
            own = field[HALO + p]
            peer = ypeer[step, p]
            row = jnp.concatenate((peer[depth_y - HALO :], own, peer[:HALO]), axis=0)
            total = eff[p] * own
            for k in range(1, 5):
                near = row[HALO + k : HALO + k + depth_y] + row[HALO - k : HALO - k + depth_y]
                near = near + pltpu.roll(own, k % width_x, 1) + pltpu.roll(own, (-k) % width_x, 1)
                total = total + (-0.5 * STENCIL[k]) * near
            acc[p] = total
            return carry

        lax.fori_loop(0, depth_z, one, 0)

    def finish(step, side):
        field = fields[step]
        z_copy(step, 1 - side).wait_recv()

        def one(p, carry):
            total = acc[p]
            for k in range(1, 5):
                total = total + (-0.5 * STENCIL[k]) * (field[HALO + p + k] + field[HALO + p - k])
            if step == 2:
                applied[p] = total
            else:
                shifted = (total - consts[0][None] * field[HALO + p]) * consts[1][None]
                if step == 0:
                    f1[HALO + p] = shifted
                else:
                    f2[HALO + p] = 2.0 * shifted - f0[HALO + p]
            return carry

        lax.fori_loop(side * lower_half, (side + 1) * lower_half, one, 0)
        if step < 2:
            z_copy(step + 1, side).start()
            y_copy(step + 1, side).start()

    def finish_both(step):
        @pl.when(g == 0)
        def _():
            finish(step, 1)
            finish(step, 0)

        @pl.when(g != 0)
        def _():
            finish(step, 0)
            finish(step, 1)

    def transposed(k):
        flat = qbuf[k].reshape(cells_dev, orbitals)
        high, low = split(flat.T)
        rows = pl.ds(pl.multiple_of(k * orbitals, orbitals), orbitals)
        qt_high[rows] = high
        qt_low[rows] = low

    loads[0].wait()
    pre(0)
    wait_ranks(tops, top_send, top_recv)
    highest = jnp.max(jnp.max(tops[...], axis=0), axis=0, keepdims=True)
    ceiling = KINETIC_TOP + jnp.broadcast_to(highest, (8, orbitals))
    consts[0] = 0.5 * (ceiling + LOWER_EDGE)
    consts[1] = 1.0 / (0.5 * (ceiling - LOWER_EDGE))
    finish_both(0)
    pre(1)
    for slot in range(2):
        loads[1 + slot].wait()
        transposed(2 * b + slot)
    finish_both(1)

    def square(p, total):
        plane = f2[HALO + p]
        return total + jnp.sum(plane * plane, axis=0)

    squares[me] = lax.fori_loop(0, depth_z, square, jnp.zeros((width_x, orbitals), jnp.float32))
    send_ranks(squares, square_send, square_recv)

    for step in range(1, nb):
        source = lax.rem(b + nb - step, nb)
        for slot in range(2):
            q_copy(step, slot).wait_recv()
            transposed(2 * source + slot)

    def product(rows, high, low):
        dot = functools.partial(jnp.dot, preferred_element_type=jnp.float32)
        first = qt_high[rows]
        return dot(first, high) + (dot(first, low) + dot(qt_low[rows], high))

    def part_copy(phase):
        return remote(
            part_out.at[phase], part_in.at[phase], part_send.at[phase], part_recv.at[phase], sub=other
        )

    mine = pl.ds(pl.multiple_of(s * half, half), half)
    theirs = pl.ds(pl.multiple_of(other * half, half), half)

    def start_gram(phase, field):
        high, low = split(field.reshape(cells_dev, orbitals))
        part_out[phase] = product(theirs, high, low)
        part_copy(phase).start()
        part_sum[phase] = product(mine, high, low)

    def chunk_rows(c):
        return pl.ds(c * chunk, chunk)

    def up_copy(phase, c, first):
        source = part_sum if first else to_high
        return remote(
            source.at[phase, chunk_rows(c)], from_low.at[phase, chunk_rows(c)],
            up_send.at[phase, c], up_recv.at[phase, c], grid=above,
        )

    def down_copy(phase, c, first):
        source = part_sum if first else to_low
        return remote(
            source.at[phase, chunk_rows(c)], from_high.at[phase, chunk_rows(c)],
            down_send.at[phase, c], down_recv.at[phase, c], grid=below,
        )

    def reduce_sub(phase):
        part_copy(phase).wait_recv()
        part_sum[phase] = part_sum[phase] + part_in[phase]

        @pl.when(g == 0)
        def _():
            for c in range(CHUNKS):
                up_copy(phase, c, True).start()

        @pl.when(g == nz - 1)
        def _():
            for c in range(CHUNKS):
                down_copy(phase, c, True).start()

    def relay_up(phase):
        @pl.when(jnp.logical_and(g > 0, g < nz - 1))
        def _():
            for c in range(CHUNKS):
                up_copy(phase, c, False).wait_recv()
                to_high[phase, chunk_rows(c)] = (
                    from_low[phase, chunk_rows(c)] + part_sum[phase, chunk_rows(c)]
                )
                up_copy(phase, c, False).start()

    def relay_down(phase):
        @pl.when(jnp.logical_and(g > 0, g < nz - 1))
        def _():
            for c in range(CHUNKS):
                down_copy(phase, c, False).wait_recv()
                to_low[phase, chunk_rows(c)] = (
                    from_high[phase, chunk_rows(c)] + part_sum[phase, chunk_rows(c)]
                )
                down_copy(phase, c, False).start()

    def relay(phase):
        @pl.when(g < nz // 2)
        def _():
            relay_up(phase)
            relay_down(phase)

        @pl.when(g >= nz // 2)
        def _():
            relay_down(phase)
            relay_up(phase)

    def out_copy(phase, c):
        rows = pl.ds(pl.multiple_of(s * half + c * chunk, chunk), chunk)
        return remote(
            out.at[phase, rows], out.at[phase, rows],
            out_send.at[phase, c], out_recv.at[phase, c], sub=other,
        )

    def conclude(phase, factor):
        for c in range(CHUNKS):
            rows = pl.ds(pl.multiple_of(s * half + c * chunk, chunk), chunk)
            own = part_sum[phase, chunk_rows(c)]

            @pl.when(g == 0)
            def _():
                down_copy(phase, c, False).wait_recv()
                out[phase, rows] = (own + from_high[phase, chunk_rows(c)]) * factor

            @pl.when(g == nz - 1)
            def _():
                up_copy(phase, c, False).wait_recv()
                out[phase, rows] = (own + from_low[phase, chunk_rows(c)]) * factor

            @pl.when(jnp.logical_and(g > 0, g < nz - 1))
            def _():
                out[phase, rows] = (
                    to_high[phase, chunk_rows(c)] + from_high[phase, chunk_rows(c)]
                ) * factor

            out_copy(phase, c).start()

    start_gram(0, f2[pl.ds(HALO, depth_z)])
    pre(2)
    reduce_sub(0)
    finish_both(2)
    start_gram(1, applied[...])
    relay(0)
    reduce_sub(1)
    wait_ranks(squares, square_send, square_recv)
    total = jnp.sum(jnp.sum(squares[...], axis=0), axis=0, keepdims=True)
    factor = lax.rsqrt(total / cells_all + EPSILON) * (1.0 / math.sqrt(cells_all))
    conclude(0, factor)
    relay(1)
    conclude(1, factor)

    for phase in range(2):
        for c in range(CHUNKS):
            out_copy(phase, c).wait()
    for step in range(3):
        for side in range(2):
            z_copy(step, side).wait_send()
            y_copy(step, side).wait_send()
    for step in range(1, nb):
        for slot in range(2):
            q_copy(step, slot).wait_send()

    def drain(step, carry):
        rank_copy(tops, top_send, top_recv, step).wait_send()
        rank_copy(squares, square_send, square_recv, step).wait_send()
        return carry

    lax.fori_loop(1, ranks, drain, 0)
    for phase in range(2):
        part_copy(phase).wait_send()

        @pl.when(g < nz - 1)
        def _():
            for c in range(CHUNKS):
                up_copy(phase, c, False).wait_send()

        @pl.when(g > 0)
        def _():
            for c in range(CHUNKS):
                down_copy(phase, c, False).wait_send()


def shards(nz, nb, filter_block, band_blocks, potential, atom_plane, block_slot):
    cells = filter_block.shape[1:]
    depth_z, depth_y, width_x, orbitals = cells
    ranks = 2 * nz
    stored = 2 * nb
    half = nb * orbitals
    cells_dev = depth_z * depth_y * width_x
    f32 = jnp.float32
    padded = pltpu.VMEM((depth_z + 2 * HALO,) + cells[1:], f32)
    whole = pltpu.VMEM(cells, f32)
    gram = pltpu.VMEM((2, half, orbitals), f32)
    dma = pltpu.SemaphoreType.DMA
    products = pl.pallas_call(
        functools.partial(kernel, nz, nb),
        out_shape=jax.ShapeDtypeStruct((2, stored * orbitals, orbitals), f32),
        in_specs=[
            pl.BlockSpec(memory_space=pl.ANY),
            pl.BlockSpec(memory_space=pl.ANY),
            pl.BlockSpec(memory_space=pltpu.VMEM),
            pl.BlockSpec(memory_space=pltpu.VMEM),
        ],
        out_specs=pl.BlockSpec(memory_space=pltpu.VMEM),
        scratch_shapes=[
            padded, padded, padded, whole, whole, whole,
            pltpu.VMEM((3,) + cells, f32),
            pltpu.VMEM((stored,) + cells, f32),
            pltpu.VMEM((stored * orbitals, cells_dev), jnp.bfloat16),
            pltpu.VMEM((stored * orbitals, cells_dev), jnp.bfloat16),
            pltpu.VMEM((2, 8, orbitals), f32),
            pltpu.VMEM((ranks, width_x, orbitals), f32),
            pltpu.VMEM((ranks, width_x, orbitals), f32),
            gram, gram, gram, gram, gram, gram, gram,
            dma((3,)),
            dma((3, 2)), dma((3, 2)), dma((3, 2)), dma((3, 2)),
            dma((nb, 2)), dma((nb, 2)),
            dma((ranks,)), dma((ranks,)), dma((ranks,)), dma((ranks,)),
            dma((2,)), dma((2,)),
            dma((2, CHUNKS)), dma((2, CHUNKS)), dma((2, CHUNKS)), dma((2, CHUNKS)),
            dma((2, CHUNKS)), dma((2, CHUNKS)),
        ],
        compiler_params=pltpu.CompilerParams(
            collective_id=0, has_side_effects=True, vmem_limit_bytes=48 * 1024 * 1024
        ),
        cost_estimate=pl.CostEstimate(
            flops=4 * cells_dev * orbitals * stored * orbitals,
            bytes_accessed=4 * orbitals * (3 * cells_dev + 2 * stored * orbitals),
            transcendentals=0,
        ),
    )(filter_block, band_blocks, potential, atom_plane.reshape(-1, 128))
    blocks = products.reshape(2, stored, orbitals, orbitals)
    placed = []
    for target in range(stored):
        block = jnp.zeros((2, orbitals, orbitals), f32)
        for k in range(stored):
            block = jnp.where(block_slot[k] == target, blocks[:, k], block)
        placed.append(block)
    placed = jnp.stack(placed, axis=1)
    return placed[0][None], placed[1][None]


def solution(mesh):
    return jax.shard_map(
        functools.partial(shards, mesh.shape["grid"], mesh.shape["band"]),
        mesh=mesh,
        in_specs=(
            P(("groups", "band"), "grid", "sub", None, None),
            P(("groups", "band"), None, "grid", "sub", None, None),
            P(("groups", "grid"), "sub", None),
            P("groups"),
            P("groups"),
        ),
        out_specs=(
            P(("groups", "band"), None, None, None),
            P(("groups", "band"), None, None, None),
        ),
        check_vma=False,
    )
```

```python
import functools
import math

import jax
import jax.numpy as jnp
from jax import lax
from jax.experimental import pallas as pl
from jax.experimental.pallas import tpu as pltpu
from jax.sharding import PartitionSpec as P

STENCIL = (-205.0 / 72.0, 8.0 / 5.0, -1.0 / 5.0, 8.0 / 315.0, -1.0 / 560.0)
LOWER_EDGE = 1.0
KINETIC_TOP = 10.0
EPSILON = 1e-06
HALO = 4
CHUNKS = 4
MESH = pl.DeviceIdType.MESH


def remote(src, dst, send_sem, recv_sem, **device):
    return pltpu.make_async_remote_copy(
        src_ref=src,
        dst_ref=dst,
        send_sem=send_sem,
        recv_sem=recv_sem,
        device_id=device,
        device_id_type=MESH,
    )


def split(value):
    high = value.astype(jnp.bfloat16)
    return high, (value - high.astype(jnp.float32)).astype(jnp.bfloat16)


def kernel(
    nz, nb, slots, x_hbm, q_hbm, pot_hbm, atoms_hbm, corr, energy,
    pot, atoms, f0, f1, f2, applied, acc, eff, ypeer, qbuf, qt_high, qt_low,
    consts, tops, squares, part_out, part_in, part_sum, from_low, from_high, to_high, to_low,
    load_sem, z_send, z_recv, y_send, y_recv, q_send, q_recv,
    top_send, top_recv, square_send, square_recv, part_send, part_recv,
    up_send, up_recv, down_send, down_recv, out_send, out_recv,
):
    g, s, b = lax.axis_index("grid"), lax.axis_index("sub"), lax.axis_index("band")
    other = 1 - s
    above, below = lax.rem(g + 1, nz), lax.rem(g + nz - 1, nz)
    depth_z, depth_y, width_x, orbitals = acc.shape
    ranks = 2 * nz
    me = 2 * g + s
    planes_all = nz * depth_z
    cells_dev = depth_z * depth_y * width_x
    cells_all = cells_dev * ranks
    half = nb * orbitals
    chunk = half // CHUNKS
    fields = (f0, f1, f2)
    lower_half = depth_z // 2

    loads = [pltpu.make_async_copy(x_hbm.at[0], f0.at[pl.ds(HALO, depth_z)], load_sem.at[0])]
    for slot in range(2):
        loads.append(
            pltpu.make_async_copy(q_hbm.at[0, slot], qbuf.at[2 * b + slot], load_sem.at[1 + slot])
        )
    loads.append(pltpu.make_async_copy(pot_hbm, pot, load_sem.at[3]))
    loads.append(pltpu.make_async_copy(atoms_hbm, atoms, load_sem.at[4]))
    for load in loads:
        load.start()

    barrier = pltpu.get_barrier_semaphore()

    def greet(step, carry):
        rank = lax.rem(me + step, ranks)
        pl.semaphore_signal(
            barrier, inc=1, device_id={"grid": rank // 2, "sub": lax.rem(rank, 2)}, device_id_type=MESH
        )
        return carry

    lax.fori_loop(1, ranks, greet, 0)
    for step in range(1, nb):
        pl.semaphore_signal(
            barrier, inc=1, device_id={"band": lax.rem(b + step, nb)}, device_id_type=MESH
        )
    pl.semaphore_wait(barrier, ranks - 1 + nb - 1)

    def z_copy(step, side):
        field = fields[step]
        if side == 0:
            src = pl.ds(HALO, HALO)
            dst = field.at[pl.ds(HALO + depth_z, HALO)]
            where = below
        else:
            src = pl.ds(depth_z, HALO)
            dst = field.at[pl.ds(0, HALO)]
            where = above
        source = field.at[src]
        if step == 0:
            source = x_hbm.at[0, pl.ds(0 if side == 0 else depth_z - HALO, HALO)]
        return remote(source, dst, z_send.at[step, side], z_recv.at[step, 1 - side], grid=where)

    def y_copy(step, side):
        planes = pl.ds(side * lower_half, lower_half)
        source = fields[step].at[pl.ds(HALO + side * lower_half, lower_half)]
        if step == 0:
            source = x_hbm.at[0, planes]
        return remote(
            source, ypeer.at[step, planes], y_send.at[step, side], y_recv.at[step, side], sub=other
        )

    def q_copy(step, slot):
        return remote(
            q_hbm.at[0, slot], qbuf.at[2 * b + slot],
            q_send.at[step - 1, slot], q_recv.at[step - 1, slot], band=lax.rem(b + step, nb),
        )

    for side in range(2):
        z_copy(0, side).start()
    for side in range(2):
        y_copy(0, side).start()
    for step in range(1, nb):
        for slot in range(2):
            q_copy(step, slot).start()

    centre_term = -0.5 * 3.0 * STENCIL[0]
    eye = lax.broadcasted_iota(jnp.int32, (width_x, width_x), 0) == lax.broadcasted_iota(
        jnp.int32, (width_x, width_x), 1
    )
    atom_total = atoms.shape[0] * atoms.shape[1]

    def plane_potential(p, top):
        hits = jnp.where(atoms[...] == g * depth_z + p, 1.0, 0.0)
        count = jnp.sum(jnp.sum(hits, axis=0, keepdims=True), axis=1, keepdims=True)
        offset = count * (planes_all / atom_total)
        for y in range(depth_y):
            row = jnp.broadcast_to(pot[p, pl.ds(y, 1), :], (width_x, width_x))
            column = jnp.sum(jnp.where(eye, row, 0.0), axis=1, keepdims=True)
            cell = jnp.broadcast_to(column + offset, (width_x, orbitals))
            top = jnp.maximum(top, cell)
            eff[p, y] = cell + centre_term
        return top

    loads[3].wait()
    loads[4].wait()
    tops[me] = lax.fori_loop(
        0, depth_z, plane_potential, jnp.full((width_x, orbitals), -jnp.inf, jnp.float32)
    )

    def rank_copy(buffer, send_sem, recv_sem, step):
        rank = lax.rem(me + step, ranks)
        return remote(
            buffer.at[me], buffer.at[me], send_sem.at[step], recv_sem.at[step],
            grid=rank // 2, sub=lax.rem(rank, 2),
        )

    def send_ranks(buffer, send_sem, recv_sem):
        def one(step, carry):
            rank_copy(buffer, send_sem, recv_sem, step).start()
            return carry

        lax.fori_loop(1, ranks, one, 0)

    def wait_ranks(buffer, send_sem, recv_sem):
        def one(step, carry):
            rank_copy(buffer, send_sem, recv_sem, step).wait_recv()
            return carry

        lax.fori_loop(1, ranks, one, 0)

    send_ranks(tops, top_send, top_recv)

    def pre(step):
        field = fields[step]
        for side in range(2):
            y_copy(step, side).wait_recv()

        def one(p, carry):
            own = field[HALO + p]
            peer = ypeer[step, p]
            row = jnp.concatenate((peer[depth_y - HALO :], own, peer[:HALO]), axis=0)
            total = eff[p] * own
            for k in range(1, 5):
                near = row[HALO + k : HALO + k + depth_y] + row[HALO - k : HALO - k + depth_y]
                near = near + pltpu.roll(own, k % width_x, 1) + pltpu.roll(own, (-k) % width_x, 1)
                total = total + (-0.5 * STENCIL[k]) * near
            acc[p] = total
            return carry

        lax.fori_loop(0, depth_z, one, 0)

    def finish(step, side):
        field = fields[step]
        z_copy(step, 1 - side).wait_recv()

        def one(p, carry):
            total = acc[p]
            for k in range(1, 5):
                total = total + (-0.5 * STENCIL[k]) * (field[HALO + p + k] + field[HALO + p - k])
            if step == 2:
                applied[p] = total
            else:
                shifted = (total - consts[0][None] * field[HALO + p]) * consts[1][None]
                if step == 0:
                    f1[HALO + p] = shifted
                else:
                    f2[HALO + p] = 2.0 * shifted - f0[HALO + p]
            return carry

        lax.fori_loop(side * lower_half, (side + 1) * lower_half, one, 0)
        if step < 2:
            z_copy(step + 1, side).start()
            y_copy(step + 1, side).start()

    def finish_both(step):
        @pl.when(g == 0)
        def _():
            finish(step, 1)
            finish(step, 0)

        @pl.when(g != 0)
        def _():
            finish(step, 0)
            finish(step, 1)

    def transposed(k):
        flat = qbuf[k].reshape(cells_dev, orbitals)
        high, low = split(flat.T)
        qt_high[k] = high
        qt_low[k] = low

    loads[0].wait()
    pre(0)
    wait_ranks(tops, top_send, top_recv)
    highest = jnp.max(jnp.max(tops[...], axis=0), axis=0, keepdims=True)
    ceiling = KINETIC_TOP + jnp.broadcast_to(highest, (8, orbitals))
    consts[0] = 0.5 * (ceiling + LOWER_EDGE)
    consts[1] = 1.0 / (0.5 * (ceiling - LOWER_EDGE))
    finish_both(0)
    pre(1)
    for slot in range(2):
        loads[1 + slot].wait()
        transposed(2 * b + slot)
    finish_both(1)

    def square(p, total):
        plane = f2[HALO + p]
        return total + jnp.sum(plane * plane, axis=0)

    squares[me] = lax.fori_loop(0, depth_z, square, jnp.zeros((width_x, orbitals), jnp.float32))
    send_ranks(squares, square_send, square_recv)

    for step in range(1, nb):
        source = lax.rem(b + nb - step, nb)
        for slot in range(2):
            q_copy(step, slot).wait_recv()
            transposed(2 * source + slot)

    def stored_at(target):
        found = jnp.int32(0)
        for k in range(2 * nb):
            found = jnp.where(slots[k] == target, jnp.int32(k), found)
        return found

    dot = functools.partial(jnp.dot, preferred_element_type=jnp.float32)

    def product(buffer, phase, base, high, low):
        for i in range(nb):
            k = stored_at(base * nb + i)
            first = qt_high[k]
            buffer[phase, pl.ds(i * orbitals, orbitals)] = dot(first, high) + (
                dot(first, low) + dot(qt_low[k], high)
            )

    def part_copy(phase):
        return remote(
            part_out.at[phase], part_in.at[phase], part_send.at[phase], part_recv.at[phase], sub=other
        )

    def start_gram(phase, field):
        high, low = split(field.reshape(cells_dev, orbitals))
        product(part_out, phase, other, high, low)
        part_copy(phase).start()
        product(part_sum, phase, s, high, low)

    def chunk_rows(c):
        return pl.ds(c * chunk, chunk)

    def up_copy(phase, c, first):
        source = part_sum if first else to_high
        return remote(
            source.at[phase, chunk_rows(c)], from_low.at[phase, chunk_rows(c)],
            up_send.at[phase, c], up_recv.at[phase, c], grid=above,
        )

    def down_copy(phase, c, first):
        source = part_sum if first else to_low
        return remote(
            source.at[phase, chunk_rows(c)], from_high.at[phase, chunk_rows(c)],
            down_send.at[phase, c], down_recv.at[phase, c], grid=below,
        )

    def reduce_sub(phase):
        part_copy(phase).wait_recv()
        part_sum[phase] = part_sum[phase] + part_in[phase]

        @pl.when(g == 0)
        def _():
            for c in range(CHUNKS):
                up_copy(phase, c, True).start()

        @pl.when(g == nz - 1)
        def _():
            for c in range(CHUNKS):
                down_copy(phase, c, True).start()

    def relay_up(phase):
        @pl.when(jnp.logical_and(g > 0, g < nz - 1))
        def _():
            for c in range(CHUNKS):
                up_copy(phase, c, False).wait_recv()
                to_high[phase, chunk_rows(c)] = (
                    from_low[phase, chunk_rows(c)] + part_sum[phase, chunk_rows(c)]
                )
                up_copy(phase, c, False).start()

    def relay_down(phase):
        @pl.when(jnp.logical_and(g > 0, g < nz - 1))
        def _():
            for c in range(CHUNKS):
                down_copy(phase, c, False).wait_recv()
                to_low[phase, chunk_rows(c)] = (
                    from_high[phase, chunk_rows(c)] + part_sum[phase, chunk_rows(c)]
                )
                down_copy(phase, c, False).start()

    def relay(phase):
        @pl.when(g < nz // 2)
        def _():
            relay_up(phase)
            relay_down(phase)

        @pl.when(g >= nz // 2)
        def _():
            relay_down(phase)
            relay_up(phase)

    outs = (corr, energy)

    def out_copy(phase, c):
        rows = pl.ds(pl.multiple_of(s * half + c * chunk, chunk), chunk)
        return remote(
            outs[phase].at[rows], outs[phase].at[rows],
            out_send.at[phase, c], out_recv.at[phase, c], sub=other,
        )

    def conclude(phase, factor):
        for c in range(CHUNKS):
            rows = pl.ds(pl.multiple_of(s * half + c * chunk, chunk), chunk)
            own = part_sum[phase, chunk_rows(c)]

            @pl.when(g == 0)
            def _():
                down_copy(phase, c, False).wait_recv()
                outs[phase][rows] = (own + from_high[phase, chunk_rows(c)]) * factor

            @pl.when(g == nz - 1)
            def _():
                up_copy(phase, c, False).wait_recv()
                outs[phase][rows] = (own + from_low[phase, chunk_rows(c)]) * factor

            @pl.when(jnp.logical_and(g > 0, g < nz - 1))
            def _():
                outs[phase][rows] = (
                    to_high[phase, chunk_rows(c)] + from_high[phase, chunk_rows(c)]
                ) * factor

            out_copy(phase, c).start()

    start_gram(0, f2[pl.ds(HALO, depth_z)])
    pre(2)
    reduce_sub(0)
    finish_both(2)
    start_gram(1, applied[...])
    relay(0)
    reduce_sub(1)
    wait_ranks(squares, square_send, square_recv)
    total = jnp.sum(jnp.sum(squares[...], axis=0), axis=0, keepdims=True)
    factor = lax.rsqrt(total / cells_all + EPSILON) * (1.0 / math.sqrt(cells_all))
    conclude(0, factor)
    relay(1)
    conclude(1, factor)

    for phase in range(2):
        for c in range(CHUNKS):
            out_copy(phase, c).wait()
    for step in range(3):
        for side in range(2):
            z_copy(step, side).wait_send()
            y_copy(step, side).wait_send()
    for step in range(1, nb):
        for slot in range(2):
            q_copy(step, slot).wait_send()

    def drain(step, carry):
        rank_copy(tops, top_send, top_recv, step).wait_send()
        rank_copy(squares, square_send, square_recv, step).wait_send()
        return carry

    lax.fori_loop(1, ranks, drain, 0)
    for phase in range(2):
        part_copy(phase).wait_send()

        @pl.when(g < nz - 1)
        def _():
            for c in range(CHUNKS):
                up_copy(phase, c, False).wait_send()

        @pl.when(g > 0)
        def _():
            for c in range(CHUNKS):
                down_copy(phase, c, False).wait_send()


def shards(nz, nb, filter_block, band_blocks, potential, atom_plane, block_slot):
    cells = filter_block.shape[1:]
    depth_z, depth_y, width_x, orbitals = cells
    ranks = 2 * nz
    stored = 2 * nb
    half = nb * orbitals
    cells_dev = depth_z * depth_y * width_x
    f32 = jnp.float32
    padded = pltpu.VMEM((depth_z + 2 * HALO,) + cells[1:], f32)
    whole = pltpu.VMEM(cells, f32)
    gram = pltpu.VMEM((2, half, orbitals), f32)
    dma = pltpu.SemaphoreType.DMA
    correlation, energy = pl.pallas_call(
        functools.partial(kernel, nz, nb),
        out_shape=(jax.ShapeDtypeStruct((stored * orbitals, orbitals), f32),) * 2,
        in_specs=[
            pl.BlockSpec(memory_space=pltpu.SMEM),
            pl.BlockSpec(memory_space=pltpu.HBM),
            pl.BlockSpec(memory_space=pltpu.HBM),
            pl.BlockSpec(memory_space=pltpu.HBM),
            pl.BlockSpec(memory_space=pltpu.HBM),
        ],
        out_specs=(pl.BlockSpec(memory_space=pltpu.VMEM),) * 2,
        scratch_shapes=[
            pltpu.VMEM(potential.shape, f32),
            pltpu.VMEM((atom_plane.shape[0] // 128, 128), jnp.int32),
            padded, padded, padded, whole, whole, whole,
            pltpu.VMEM((3,) + cells, f32),
            pltpu.VMEM((stored,) + cells, f32),
            pltpu.VMEM((stored, orbitals, cells_dev), jnp.bfloat16),
            pltpu.VMEM((stored, orbitals, cells_dev), jnp.bfloat16),
            pltpu.VMEM((2, 8, orbitals), f32),
            pltpu.VMEM((ranks, width_x, orbitals), f32),
            pltpu.VMEM((ranks, width_x, orbitals), f32),
            gram, gram, gram, gram, gram, gram, gram,
            dma((5,)),
            dma((3, 2)), dma((3, 2)), dma((3, 2)), dma((3, 2)),
            dma((nb, 2)), dma((nb, 2)),
            dma((ranks,)), dma((ranks,)), dma((ranks,)), dma((ranks,)),
            dma((2,)), dma((2,)),
            dma((2, CHUNKS)), dma((2, CHUNKS)), dma((2, CHUNKS)), dma((2, CHUNKS)),
            dma((2, CHUNKS)), dma((2, CHUNKS)),
        ],
        compiler_params=pltpu.CompilerParams(
            collective_id=0, has_side_effects=True, vmem_limit_bytes=60 * 1024 * 1024
        ),
        cost_estimate=pl.CostEstimate(
            flops=4 * cells_dev * orbitals * stored * orbitals,
            bytes_accessed=4 * orbitals * (3 * cells_dev + 2 * stored * orbitals),
            transcendentals=0,
        ),
    )(block_slot, filter_block, band_blocks, potential, atom_plane.reshape(-1, 128))
    shape = (1, stored, orbitals, orbitals)
    return correlation.reshape(shape), energy.reshape(shape)


def solution(mesh):
    return jax.shard_map(
        functools.partial(shards, mesh.shape["grid"], mesh.shape["band"]),
        mesh=mesh,
        in_specs=(
            P(("groups", "band"), "grid", "sub", None, None),
            P(("groups", "band"), None, "grid", "sub", None, None),
            P(("groups", "grid"), "sub", None),
            P("groups"),
            P("groups"),
        ),
        out_specs=(
            P(("groups", "band"), None, None, None),
            P(("groups", "band"), None, None, None),
        ),
        check_vma=False,
    )
```

```python
import functools
import math

import jax
import jax.numpy as jnp
from jax import lax
from jax.experimental import pallas as pl
from jax.experimental.pallas import tpu as pltpu
from jax.sharding import PartitionSpec as P

STENCIL = (-205.0 / 72.0, 8.0 / 5.0, -1.0 / 5.0, 8.0 / 315.0, -1.0 / 560.0)
LOWER_EDGE = 1.0
KINETIC_TOP = 10.0
EPSILON = 1e-06
HALO = 4
CHUNKS = 4
MESH = pl.DeviceIdType.MESH


def remote(src, dst, send_sem, recv_sem, **device):
    return pltpu.make_async_remote_copy(
        src_ref=src,
        dst_ref=dst,
        send_sem=send_sem,
        recv_sem=recv_sem,
        device_id=device,
        device_id_type=MESH,
    )


def split(value):
    high = value.astype(jnp.bfloat16)
    return high, (value - high.astype(jnp.float32)).astype(jnp.bfloat16)


def kernel(
    nz, nb, slots, x_hbm, q_hbm, pot_hbm, atoms_hbm, out,
    pot, atoms, f0, f1, f2, applied, acc, eff, ypeer, qbuf, qt_high, qt_low,
    consts, tops, squares, part_out, part_in, part_sum, from_low, from_high, to_high, to_low,
    load_sem, z_send, z_recv, y_send, y_recv, q_send, q_recv,
    top_send, top_recv, square_send, square_recv, part_send, part_recv,
    up_send, up_recv, down_send, down_recv, out_send, out_recv,
):
    g, s, b = lax.axis_index("grid"), lax.axis_index("sub"), lax.axis_index("band")
    other = 1 - s
    above, below = lax.rem(g + 1, nz), lax.rem(g + nz - 1, nz)
    depth_z, depth_y, width_x, orbitals = acc.shape
    ranks = 2 * nz
    me = 2 * g + s
    planes_all = nz * depth_z
    cells_dev = depth_z * depth_y * width_x
    cells_all = cells_dev * ranks
    half = nb * orbitals
    chunk = half // CHUNKS
    fields = (f0, f1, f2)
    lower_half = depth_z // 2

    loads = [pltpu.make_async_copy(x_hbm.at[0], f0.at[pl.ds(HALO, depth_z)], load_sem.at[0])]
    for slot in range(2):
        loads.append(
            pltpu.make_async_copy(q_hbm.at[0, slot], qbuf.at[2 * b + slot], load_sem.at[1 + slot])
        )
    loads.append(pltpu.make_async_copy(pot_hbm, pot, load_sem.at[3]))
    loads.append(pltpu.make_async_copy(atoms_hbm, atoms, load_sem.at[4]))
    for load in loads:
        load.start()

    barrier = pltpu.get_barrier_semaphore()

    def greet(step, carry):
        rank = lax.rem(me + step, ranks)
        pl.semaphore_signal(
            barrier, inc=1, device_id={"grid": rank // 2, "sub": lax.rem(rank, 2)}, device_id_type=MESH
        )
        return carry

    lax.fori_loop(1, ranks, greet, 0)
    for step in range(1, nb):
        pl.semaphore_signal(
            barrier, inc=1, device_id={"band": lax.rem(b + step, nb)}, device_id_type=MESH
        )
    pl.semaphore_wait(barrier, ranks - 1 + nb - 1)

    def z_copy(step, side):
        field = fields[step]
        if side == 0:
            src = pl.ds(HALO, HALO)
            dst = field.at[pl.ds(HALO + depth_z, HALO)]
            where = below
        else:
            src = pl.ds(depth_z, HALO)
            dst = field.at[pl.ds(0, HALO)]
            where = above
        source = field.at[src]
        if step == 0:
            source = x_hbm.at[0, pl.ds(0 if side == 0 else depth_z - HALO, HALO)]
        return remote(source, dst, z_send.at[step, side], z_recv.at[step, 1 - side], grid=where)

    def y_copy(step, side):
        planes = pl.ds(side * lower_half, lower_half)
        source = fields[step].at[pl.ds(HALO + side * lower_half, lower_half)]
        if step == 0:
            source = x_hbm.at[0, planes]
        return remote(
            source, ypeer.at[step, planes], y_send.at[step, side], y_recv.at[step, side], sub=other
        )

    def q_copy(step, slot):
        return remote(
            q_hbm.at[0, slot], qbuf.at[2 * b + slot],
            q_send.at[step - 1, slot], q_recv.at[step - 1, slot], band=lax.rem(b + step, nb),
        )

    for side in range(2):
        z_copy(0, side).start()
    for side in range(2):
        y_copy(0, side).start()
    for step in range(1, nb):
        for slot in range(2):
            q_copy(step, slot).start()

    centre_term = -0.5 * 3.0 * STENCIL[0]
    eye = lax.broadcasted_iota(jnp.int32, (width_x, width_x), 0) == lax.broadcasted_iota(
        jnp.int32, (width_x, width_x), 1
    )
    atom_total = atoms.shape[0] * atoms.shape[1]

    def plane_potential(p, top):
        hits = jnp.where(atoms[...] == g * depth_z + p, 1.0, 0.0)
        count = jnp.sum(jnp.sum(hits, axis=0, keepdims=True), axis=1, keepdims=True)
        offset = count * (planes_all / atom_total)
        for y in range(depth_y):
            row = jnp.broadcast_to(pot[p, pl.ds(y, 1), :], (width_x, width_x))
            column = jnp.sum(jnp.where(eye, row, 0.0), axis=1, keepdims=True)
            cell = jnp.broadcast_to(column + offset, (width_x, orbitals))
            top = jnp.maximum(top, cell)
            eff[p, y] = cell + centre_term
        return top

    loads[3].wait()
    loads[4].wait()
    tops[me] = lax.fori_loop(
        0, depth_z, plane_potential, jnp.full((width_x, orbitals), -jnp.inf, jnp.float32)
    )

    def rank_copy(buffer, send_sem, recv_sem, step):
        rank = lax.rem(me + step, ranks)
        return remote(
            buffer.at[me], buffer.at[me], send_sem.at[step], recv_sem.at[step],
            grid=rank // 2, sub=lax.rem(rank, 2),
        )

    def send_ranks(buffer, send_sem, recv_sem):
        def one(step, carry):
            rank_copy(buffer, send_sem, recv_sem, step).start()
            return carry

        lax.fori_loop(1, ranks, one, 0)

    def wait_ranks(buffer, send_sem, recv_sem):
        def one(step, carry):
            rank_copy(buffer, send_sem, recv_sem, step).wait_recv()
            return carry

        lax.fori_loop(1, ranks, one, 0)

    send_ranks(tops, top_send, top_recv)

    def pre(step):
        field = fields[step]
        for side in range(2):
            y_copy(step, side).wait_recv()

        def one(p, carry):
            own = field[HALO + p]
            peer = ypeer[step, p]
            row = jnp.concatenate((peer[depth_y - HALO :], own, peer[:HALO]), axis=0)
            total = eff[p] * own
            for k in range(1, 5):
                near = row[HALO + k : HALO + k + depth_y] + row[HALO - k : HALO - k + depth_y]
                near = near + pltpu.roll(own, k % width_x, 1) + pltpu.roll(own, (-k) % width_x, 1)
                total = total + (-0.5 * STENCIL[k]) * near
            acc[p] = total
            return carry

        lax.fori_loop(0, depth_z, one, 0)

    def finish(step, side):
        field = fields[step]
        z_copy(step, 1 - side).wait_recv()

        def one(p, carry):
            total = acc[p]
            for k in range(1, 5):
                total = total + (-0.5 * STENCIL[k]) * (field[HALO + p + k] + field[HALO + p - k])
            if step == 2:
                applied[p] = total
            else:
                shifted = (total - consts[0][None] * field[HALO + p]) * consts[1][None]
                if step == 0:
                    f1[HALO + p] = shifted
                else:
                    f2[HALO + p] = 2.0 * shifted - f0[HALO + p]
            return carry

        lax.fori_loop(side * lower_half, (side + 1) * lower_half, one, 0)
        if step < 2:
            z_copy(step + 1, side).start()
            y_copy(step + 1, side).start()

    def finish_both(step):
        @pl.when(g == 0)
        def _():
            finish(step, 1)
            finish(step, 0)

        @pl.when(g != 0)
        def _():
            finish(step, 0)
            finish(step, 1)

    def transposed(k):
        flat = qbuf[k].reshape(cells_dev, orbitals)
        high, low = split(flat.T)
        qt_high[k] = high
        qt_low[k] = low

    loads[0].wait()
    pre(0)
    wait_ranks(tops, top_send, top_recv)
    highest = jnp.max(jnp.max(tops[...], axis=0), axis=0, keepdims=True)
    ceiling = KINETIC_TOP + jnp.broadcast_to(highest, (8, orbitals))
    consts[0] = 0.5 * (ceiling + LOWER_EDGE)
    consts[1] = 1.0 / (0.5 * (ceiling - LOWER_EDGE))
    finish_both(0)
    pre(1)
    for slot in range(2):
        loads[1 + slot].wait()
        transposed(2 * b + slot)
    finish_both(1)

    def square(p, total):
        plane = f2[HALO + p]
        return total + jnp.sum(plane * plane, axis=0)

    squares[me] = lax.fori_loop(0, depth_z, square, jnp.zeros((width_x, orbitals), jnp.float32))
    send_ranks(squares, square_send, square_recv)

    for step in range(1, nb):
        source = lax.rem(b + nb - step, nb)
        for slot in range(2):
            q_copy(step, slot).wait_recv()
            transposed(2 * source + slot)

    def stored_at(target):
        found = jnp.int32(0)
        for k in range(2 * nb):
            found = jnp.where(slots[k] == target, jnp.int32(k), found)
        return found

    dot = functools.partial(jnp.dot, preferred_element_type=jnp.float32)

    def product(buffer, phase, base, high, low):
        for i in range(nb):
            k = stored_at(base * nb + i)
            first = qt_high[k]
            buffer[phase, pl.ds(i * orbitals, orbitals)] = dot(first, high) + (
                dot(first, low) + dot(qt_low[k], high)
            )

    def part_copy(phase):
        return remote(
            part_out.at[phase], part_in.at[phase], part_send.at[phase], part_recv.at[phase], sub=other
        )

    def start_gram(phase, field):
        high, low = split(field.reshape(cells_dev, orbitals))
        product(part_out, phase, other, high, low)
        part_copy(phase).start()
        product(part_sum, phase, s, high, low)

    def chunk_rows(c):
        return pl.ds(c * chunk, chunk)

    def up_copy(phase, c, first):
        source = part_sum if first else to_high
        return remote(
            source.at[phase, chunk_rows(c)], from_low.at[phase, chunk_rows(c)],
            up_send.at[phase, c], up_recv.at[phase, c], grid=above,
        )

    def down_copy(phase, c, first):
        source = part_sum if first else to_low
        return remote(
            source.at[phase, chunk_rows(c)], from_high.at[phase, chunk_rows(c)],
            down_send.at[phase, c], down_recv.at[phase, c], grid=below,
        )

    def reduce_sub(phase):
        part_copy(phase).wait_recv()
        part_sum[phase] = part_sum[phase] + part_in[phase]

        @pl.when(g == 0)
        def _():
            for c in range(CHUNKS):
                up_copy(phase, c, True).start()

        @pl.when(g == nz - 1)
        def _():
            for c in range(CHUNKS):
                down_copy(phase, c, True).start()

    def relay_up(phase):
        @pl.when(jnp.logical_and(g > 0, g < nz - 1))
        def _():
            for c in range(CHUNKS):
                up_copy(phase, c, False).wait_recv()
                to_high[phase, chunk_rows(c)] = (
                    from_low[phase, chunk_rows(c)] + part_sum[phase, chunk_rows(c)]
                )
                up_copy(phase, c, False).start()

    def relay_down(phase):
        @pl.when(jnp.logical_and(g > 0, g < nz - 1))
        def _():
            for c in range(CHUNKS):
                down_copy(phase, c, False).wait_recv()
                to_low[phase, chunk_rows(c)] = (
                    from_high[phase, chunk_rows(c)] + part_sum[phase, chunk_rows(c)]
                )
                down_copy(phase, c, False).start()

    def relay(phase):
        @pl.when(g < nz // 2)
        def _():
            relay_up(phase)
            relay_down(phase)

        @pl.when(g >= nz // 2)
        def _():
            relay_down(phase)
            relay_up(phase)

    def out_copy(phase, c):
        rows = pl.ds(pl.multiple_of(s * half + c * chunk, chunk), chunk)
        return remote(
            out.at[phase, rows], out.at[phase, rows],
            out_send.at[phase, c], out_recv.at[phase, c], sub=other,
        )

    def conclude(phase, factor):
        for c in range(CHUNKS):
            rows = pl.ds(pl.multiple_of(s * half + c * chunk, chunk), chunk)
            own = part_sum[phase, chunk_rows(c)]

            @pl.when(g == 0)
            def _():
                down_copy(phase, c, False).wait_recv()
                out[phase, rows] = (own + from_high[phase, chunk_rows(c)]) * factor

            @pl.when(g == nz - 1)
            def _():
                up_copy(phase, c, False).wait_recv()
                out[phase, rows] = (own + from_low[phase, chunk_rows(c)]) * factor

            @pl.when(jnp.logical_and(g > 0, g < nz - 1))
            def _():
                out[phase, rows] = (
                    to_high[phase, chunk_rows(c)] + from_high[phase, chunk_rows(c)]
                ) * factor

            out_copy(phase, c).start()

    start_gram(0, f2[pl.ds(HALO, depth_z)])
    pre(2)
    reduce_sub(0)
    wait_ranks(squares, square_send, square_recv)
    total = jnp.sum(jnp.sum(squares[...], axis=0), axis=0, keepdims=True)
    factor = lax.rsqrt(total / cells_all + EPSILON)
    relay(0)
    finish_both(2)
    start_gram(1, applied[...])
    conclude(0, factor)
    reduce_sub(1)
    relay(1)
    conclude(1, factor)

    for phase in range(2):
        for c in range(CHUNKS):
            out_copy(phase, c).wait()
    for step in range(3):
        for side in range(2):
            z_copy(step, side).wait_send()
            y_copy(step, side).wait_send()
    for step in range(1, nb):
        for slot in range(2):
            q_copy(step, slot).wait_send()

    def drain(step, carry):
        rank_copy(tops, top_send, top_recv, step).wait_send()
        rank_copy(squares, square_send, square_recv, step).wait_send()
        return carry

    lax.fori_loop(1, ranks, drain, 0)
    for phase in range(2):
        part_copy(phase).wait_send()

        @pl.when(g < nz - 1)
        def _():
            for c in range(CHUNKS):
                up_copy(phase, c, False).wait_send()

        @pl.when(g > 0)
        def _():
            for c in range(CHUNKS):
                down_copy(phase, c, False).wait_send()


def shards(nz, nb, filter_block, band_blocks, potential, atom_plane, block_slot):
    cells = filter_block.shape[1:]
    depth_z, depth_y, width_x, orbitals = cells
    ranks = 2 * nz
    stored = 2 * nb
    half = nb * orbitals
    cells_dev = depth_z * depth_y * width_x
    f32 = jnp.float32
    padded = pltpu.VMEM((depth_z + 2 * HALO,) + cells[1:], f32)
    whole = pltpu.VMEM(cells, f32)
    gram = pltpu.VMEM((2, half, orbitals), f32)
    dma = pltpu.SemaphoreType.DMA
    products = pl.pallas_call(
        functools.partial(kernel, nz, nb),
        out_shape=jax.ShapeDtypeStruct((2, stored * orbitals, orbitals), f32),
        in_specs=[
            pl.BlockSpec(memory_space=pltpu.SMEM),
            pl.BlockSpec(memory_space=pltpu.HBM),
            pl.BlockSpec(memory_space=pltpu.HBM),
            pl.BlockSpec(memory_space=pltpu.HBM),
            pl.BlockSpec(memory_space=pltpu.HBM),
        ],
        out_specs=pl.BlockSpec(memory_space=pltpu.VMEM),
        scratch_shapes=[
            pltpu.VMEM(potential.shape, f32),
            pltpu.VMEM((atom_plane.shape[0] // 128, 128), jnp.int32),
            padded, padded, padded, whole, whole, whole,
            pltpu.VMEM((3,) + cells, f32),
            pltpu.VMEM((stored,) + cells, f32),
            pltpu.VMEM((stored, orbitals, cells_dev), jnp.bfloat16),
            pltpu.VMEM((stored, orbitals, cells_dev), jnp.bfloat16),
            pltpu.VMEM((2, 8, orbitals), f32),
            pltpu.VMEM((ranks, width_x, orbitals), f32),
            pltpu.VMEM((ranks, width_x, orbitals), f32),
            gram, gram, gram, gram, gram, gram, gram,
            dma((5,)),
            dma((3, 2)), dma((3, 2)), dma((3, 2)), dma((3, 2)),
            dma((nb, 2)), dma((nb, 2)),
            dma((ranks,)), dma((ranks,)), dma((ranks,)), dma((ranks,)),
            dma((2,)), dma((2,)),
            dma((2, CHUNKS)), dma((2, CHUNKS)), dma((2, CHUNKS)), dma((2, CHUNKS)),
            dma((2, CHUNKS)), dma((2, CHUNKS)),
        ],
        compiler_params=pltpu.CompilerParams(
            collective_id=0, has_side_effects=True, vmem_limit_bytes=60 * 1024 * 1024
        ),
        cost_estimate=pl.CostEstimate(
            flops=4 * cells_dev * orbitals * stored * orbitals,
            bytes_accessed=4 * orbitals * (3 * cells_dev + 2 * stored * orbitals),
            transcendentals=0,
        ),
    )(block_slot, filter_block, band_blocks, potential, atom_plane.reshape(-1, 128))
    shape = (1, stored, orbitals, orbitals)
    norm_factor = 1.0 / math.sqrt(cells_dev * ranks)
    return (products[0] * norm_factor).reshape(shape), (products[1] * norm_factor).reshape(shape)


def solution(mesh):
    return jax.shard_map(
        functools.partial(shards, mesh.shape["grid"], mesh.shape["band"]),
        mesh=mesh,
        in_specs=(
            P(("groups", "band"), "grid", "sub", None, None),
            P(("groups", "band"), None, "grid", "sub", None, None),
            P(("groups", "grid"), "sub", None),
            P("groups"),
            P("groups"),
        ),
        out_specs=(
            P(("groups", "band"), None, None, None),
            P(("groups", "band"), None, None, None),
        ),
        check_vma=False,
    )
```

```python
import functools
import math

import jax
import jax.numpy as jnp
from jax import lax
from jax.experimental import pallas as pl
from jax.experimental.pallas import tpu as pltpu
from jax.sharding import PartitionSpec as P

STENCIL = (-205.0 / 72.0, 8.0 / 5.0, -1.0 / 5.0, 8.0 / 315.0, -1.0 / 560.0)
LOWER_EDGE = 1.0
KINETIC_TOP = 10.0
EPSILON = 1e-06
HALO = 4
CHUNKS = 4
MESH = pl.DeviceIdType.MESH


def remote(src, dst, send_sem, recv_sem, **device):
    return pltpu.make_async_remote_copy(
        src_ref=src,
        dst_ref=dst,
        send_sem=send_sem,
        recv_sem=recv_sem,
        device_id=device,
        device_id_type=MESH,
    )


def split(value):
    high = value.astype(jnp.bfloat16)
    return high, (value - high.astype(jnp.float32)).astype(jnp.bfloat16)


def kernel(
    nz, nb, slots, x_hbm, q_hbm, pot_hbm, atoms_hbm, out,
    pot, atoms, f0, f1, f2, applied, acc, eff, ypeer, qbuf, qt_high, qt_low,
    consts, tops, squares, part_out, part_in, part_sum, from_low, from_high, to_high, to_low,
    load_sem, z_send, z_recv, y_send, y_recv, q_send, q_recv,
    top_send, top_recv, square_send, square_recv, part_send, part_recv,
    up_send, up_recv, down_send, down_recv, out_send, out_recv,
):
    g, s, b = lax.axis_index("grid"), lax.axis_index("sub"), lax.axis_index("band")
    other = 1 - s
    above, below = lax.rem(g + 1, nz), lax.rem(g + nz - 1, nz)
    depth_z, depth_y, width_x, orbitals = acc.shape
    ranks = 2 * nz
    me = 2 * g + s
    planes_all = nz * depth_z
    cells_dev = depth_z * depth_y * width_x
    cells_all = cells_dev * ranks
    half = nb * orbitals
    chunk = half // CHUNKS
    fields = (f0, f1, f2)
    lower_half = depth_z // 2

    loads = [pltpu.make_async_copy(x_hbm.at[0], f0.at[pl.ds(HALO, depth_z)], load_sem.at[0])]
    for slot in range(2):
        loads.append(
            pltpu.make_async_copy(q_hbm.at[0, slot], qbuf.at[2 * b + slot], load_sem.at[1 + slot])
        )
    loads.append(pltpu.make_async_copy(pot_hbm, pot, load_sem.at[3]))
    loads.append(pltpu.make_async_copy(atoms_hbm, atoms, load_sem.at[4]))
    for load in loads:
        load.start()

    barrier = pltpu.get_barrier_semaphore()

    def greet(step, carry):
        rank = lax.rem(me + step, ranks)
        pl.semaphore_signal(
            barrier, inc=1, device_id={"grid": rank // 2, "sub": lax.rem(rank, 2)}, device_id_type=MESH
        )
        return carry

    lax.fori_loop(1, ranks, greet, 0)
    for step in range(1, nb):
        pl.semaphore_signal(
            barrier, inc=1, device_id={"band": lax.rem(b + step, nb)}, device_id_type=MESH
        )
    pl.semaphore_wait(barrier, ranks - 1 + nb - 1)

    def z_copy(step, side):
        field = fields[step]
        if side == 0:
            src = pl.ds(HALO, HALO)
            dst = field.at[pl.ds(HALO + depth_z, HALO)]
            where = below
        else:
            src = pl.ds(depth_z, HALO)
            dst = field.at[pl.ds(0, HALO)]
            where = above
        source = field.at[src]
        if step == 0:
            source = x_hbm.at[0, pl.ds(0 if side == 0 else depth_z - HALO, HALO)]
        return remote(source, dst, z_send.at[step, side], z_recv.at[step, 1 - side], grid=where)

    def y_copy(step, side):
        planes = pl.ds(side * lower_half, lower_half)
        source = fields[step].at[pl.ds(HALO + side * lower_half, lower_half)]
        if step == 0:
            source = x_hbm.at[0, planes]
        return remote(
            source, ypeer.at[step, planes], y_send.at[step, side], y_recv.at[step, side], sub=other
        )

    def q_copy(step, slot):
        return remote(
            q_hbm.at[0, slot], qbuf.at[2 * b + slot],
            q_send.at[step - 1, slot], q_recv.at[step - 1, slot], band=lax.rem(b + step, nb),
        )

    for side in range(2):
        z_copy(0, side).start()
    for side in range(2):
        y_copy(0, side).start()
    for step in range(1, nb):
        for slot in range(2):
            q_copy(step, slot).start()

    centre_term = -0.5 * 3.0 * STENCIL[0]
    eye = lax.broadcasted_iota(jnp.int32, (width_x, width_x), 0) == lax.broadcasted_iota(
        jnp.int32, (width_x, width_x), 1
    )
    atom_total = atoms.shape[0] * atoms.shape[1]

    def plane_potential(p, top):
        hits = jnp.where(atoms[...] == g * depth_z + p, 1.0, 0.0)
        count = jnp.sum(jnp.sum(hits, axis=0, keepdims=True), axis=1, keepdims=True)
        offset = count * (planes_all / atom_total)
        for y in range(depth_y):
            row = jnp.broadcast_to(pot[p, pl.ds(y, 1), :], (width_x, width_x))
            column = jnp.sum(jnp.where(eye, row, 0.0), axis=1, keepdims=True)
            cell = jnp.broadcast_to(column + offset, (width_x, orbitals))
            top = jnp.maximum(top, cell)
            eff[p, y] = cell + centre_term
        return top

    loads[3].wait()
    loads[4].wait()
    tops[me] = lax.fori_loop(
        0, depth_z, plane_potential, jnp.full((width_x, orbitals), -jnp.inf, jnp.float32)
    )

    def rank_copy(buffer, send_sem, recv_sem, step):
        rank = lax.rem(me + step, ranks)
        return remote(
            buffer.at[me], buffer.at[me], send_sem.at[step], recv_sem.at[step],
            grid=rank // 2, sub=lax.rem(rank, 2),
        )

    def send_ranks(buffer, send_sem, recv_sem):
        def one(step, carry):
            rank_copy(buffer, send_sem, recv_sem, step).start()
            return carry

        lax.fori_loop(1, ranks, one, 0)

    def wait_ranks(buffer, send_sem, recv_sem):
        def one(step, carry):
            rank_copy(buffer, send_sem, recv_sem, step).wait_recv()
            return carry

        lax.fori_loop(1, ranks, one, 0)

    send_ranks(tops, top_send, top_recv)

    def pre(step):
        field = fields[step]
        for side in range(2):
            y_copy(step, side).wait_recv()

        def one(p, carry):
            own = field[HALO + p]
            peer = ypeer[step, p]
            row = jnp.concatenate((peer[depth_y - HALO :], own, peer[:HALO]), axis=0)
            total = eff[p] * own
            for k in range(1, 5):
                near = row[HALO + k : HALO + k + depth_y] + row[HALO - k : HALO - k + depth_y]
                near = near + pltpu.roll(own, k % width_x, 1) + pltpu.roll(own, (-k) % width_x, 1)
                total = total + (-0.5 * STENCIL[k]) * near
            acc[p] = total
            return carry

        lax.fori_loop(0, depth_z, one, 0)

    def finish(step, side):
        field = fields[step]
        z_copy(step, 1 - side).wait_recv()

        def one(p, carry):
            total = acc[p]
            for k in range(1, 5):
                total = total + (-0.5 * STENCIL[k]) * (field[HALO + p + k] + field[HALO + p - k])
            if step == 2:
                applied[p] = total
            else:
                shifted = (total - consts[0][None] * field[HALO + p]) * consts[1][None]
                if step == 0:
                    f1[HALO + p] = shifted
                else:
                    f2[HALO + p] = 2.0 * shifted - f0[HALO + p]
            return carry

        lax.fori_loop(side * lower_half, (side + 1) * lower_half, one, 0)
        if step < 2:
            z_copy(step + 1, side).start()
            y_copy(step + 1, side).start()

    def finish_both(step):
        @pl.when(g == 0)
        def _():
            finish(step, 1)
            finish(step, 0)

        @pl.when(g != 0)
        def _():
            finish(step, 0)
            finish(step, 1)

    def transposed(k):
        flat = qbuf[k].reshape(cells_dev, orbitals)
        high, low = split(flat.T)
        qt_high[k] = high
        qt_low[k] = low

    loads[0].wait()
    pre(0)
    wait_ranks(tops, top_send, top_recv)
    highest = jnp.max(jnp.max(tops[...], axis=0), axis=0, keepdims=True)
    ceiling = KINETIC_TOP + jnp.broadcast_to(highest, (8, orbitals))
    consts[0] = 0.5 * (ceiling + LOWER_EDGE)
    consts[1] = 1.0 / (0.5 * (ceiling - LOWER_EDGE))
    finish_both(0)
    pre(1)
    for slot in range(2):
        loads[1 + slot].wait()
        transposed(2 * b + slot)
    finish_both(1)

    def square(p, total):
        plane = f2[HALO + p]
        return total + jnp.sum(plane * plane, axis=0)

    squares[me] = lax.fori_loop(0, depth_z, square, jnp.zeros((width_x, orbitals), jnp.float32))
    send_ranks(squares, square_send, square_recv)

    for step in range(1, nb):
        source = lax.rem(b + nb - step, nb)
        for slot in range(2):
            q_copy(step, slot).wait_recv()
            transposed(2 * source + slot)

    def stored_at(target):
        found = jnp.int32(0)
        for k in range(2 * nb):
            found = jnp.where(slots[k] == target, jnp.int32(k), found)
        return found

    dot = functools.partial(jnp.dot, preferred_element_type=jnp.float32)

    def product(buffer, phase, base, high, low):
        for i in range(nb):
            k = stored_at(base * nb + i)
            first = qt_high[k]
            buffer[phase, pl.ds(i * orbitals, orbitals)] = dot(first, high) + (
                dot(first, low) + dot(qt_low[k], high)
            )

    def part_copy(phase):
        return remote(
            part_out.at[phase], part_in.at[phase], part_send.at[phase], part_recv.at[phase], sub=other
        )

    def start_gram(phase, field):
        high, low = split(field.reshape(cells_dev, orbitals))
        product(part_out, phase, other, high, low)
        part_copy(phase).start()
        product(part_sum, phase, s, high, low)

    def chunk_rows(c):
        return pl.ds(c * chunk, chunk)

    def up_copy(phase, c, first):
        source = part_sum if first else to_high
        return remote(
            source.at[phase, chunk_rows(c)], from_low.at[phase, chunk_rows(c)],
            up_send.at[phase, c], up_recv.at[phase, c], grid=above,
        )

    def down_copy(phase, c, first):
        source = part_sum if first else to_low
        return remote(
            source.at[phase, chunk_rows(c)], from_high.at[phase, chunk_rows(c)],
            down_send.at[phase, c], down_recv.at[phase, c], grid=below,
        )

    def reduce_sub(phase):
        part_copy(phase).wait_recv()
        part_sum[phase] = part_sum[phase] + part_in[phase]

        @pl.when(g == 0)
        def _():
            for c in range(CHUNKS):
                up_copy(phase, c, True).start()

        @pl.when(g == nz - 1)
        def _():
            for c in range(CHUNKS):
                down_copy(phase, c, True).start()

    def relay_up(phase):
        @pl.when(jnp.logical_and(g > 0, g < nz - 1))
        def _():
            for c in range(CHUNKS):
                up_copy(phase, c, False).wait_recv()
                to_high[phase, chunk_rows(c)] = (
                    from_low[phase, chunk_rows(c)] + part_sum[phase, chunk_rows(c)]
                )
                up_copy(phase, c, False).start()

    def relay_down(phase):
        @pl.when(jnp.logical_and(g > 0, g < nz - 1))
        def _():
            for c in range(CHUNKS):
                down_copy(phase, c, False).wait_recv()
                to_low[phase, chunk_rows(c)] = (
                    from_high[phase, chunk_rows(c)] + part_sum[phase, chunk_rows(c)]
                )
                down_copy(phase, c, False).start()

    def relay(phase):
        @pl.when(g < nz // 2)
        def _():
            relay_up(phase)
            relay_down(phase)

        @pl.when(g >= nz // 2)
        def _():
            relay_down(phase)
            relay_up(phase)

    def out_copy(phase, c):
        rows = pl.ds(pl.multiple_of(s * half + c * chunk, chunk), chunk)
        return remote(
            out.at[phase, rows], out.at[phase, rows],
            out_send.at[phase, c], out_recv.at[phase, c], sub=other,
        )

    def conclude(phase, factor):
        for c in range(CHUNKS):
            rows = pl.ds(pl.multiple_of(s * half + c * chunk, chunk), chunk)
            own = part_sum[phase, chunk_rows(c)]

            @pl.when(g == 0)
            def _():
                down_copy(phase, c, False).wait_recv()
                out[phase, rows] = (own + from_high[phase, chunk_rows(c)]) * factor

            @pl.when(g == nz - 1)
            def _():
                up_copy(phase, c, False).wait_recv()
                out[phase, rows] = (own + from_low[phase, chunk_rows(c)]) * factor

            @pl.when(jnp.logical_and(g > 0, g < nz - 1))
            def _():
                out[phase, rows] = (
                    to_high[phase, chunk_rows(c)] + from_high[phase, chunk_rows(c)]
                ) * factor

            out_copy(phase, c).start()

    start_gram(0, f2[pl.ds(HALO, depth_z)])
    pre(2)
    reduce_sub(0)
    wait_ranks(squares, square_send, square_recv)
    total = jnp.sum(jnp.sum(squares[...], axis=0), axis=0, keepdims=True)
    factor = lax.rsqrt(total / cells_all + EPSILON)
    finish_both(2)
    start_gram(1, applied[...])
    relay(0)
    reduce_sub(1)
    relay(1)
    conclude(0, factor)
    conclude(1, factor)

    for phase in range(2):
        for c in range(CHUNKS):
            out_copy(phase, c).wait()
    for step in range(3):
        for side in range(2):
            z_copy(step, side).wait_send()
            y_copy(step, side).wait_send()
    for step in range(1, nb):
        for slot in range(2):
            q_copy(step, slot).wait_send()

    def drain(step, carry):
        rank_copy(tops, top_send, top_recv, step).wait_send()
        rank_copy(squares, square_send, square_recv, step).wait_send()
        return carry

    lax.fori_loop(1, ranks, drain, 0)
    for phase in range(2):
        part_copy(phase).wait_send()

        @pl.when(g < nz - 1)
        def _():
            for c in range(CHUNKS):
                up_copy(phase, c, False).wait_send()

        @pl.when(g > 0)
        def _():
            for c in range(CHUNKS):
                down_copy(phase, c, False).wait_send()


def shards(nz, nb, filter_block, band_blocks, potential, atom_plane, block_slot):
    cells = filter_block.shape[1:]
    depth_z, depth_y, width_x, orbitals = cells
    ranks = 2 * nz
    stored = 2 * nb
    half = nb * orbitals
    cells_dev = depth_z * depth_y * width_x
    f32 = jnp.float32
    padded = pltpu.VMEM((depth_z + 2 * HALO,) + cells[1:], f32)
    whole = pltpu.VMEM(cells, f32)
    gram = pltpu.VMEM((2, half, orbitals), f32)
    dma = pltpu.SemaphoreType.DMA
    products = pl.pallas_call(
        functools.partial(kernel, nz, nb),
        out_shape=jax.ShapeDtypeStruct((2, stored * orbitals, orbitals), f32),
        in_specs=[
            pl.BlockSpec(memory_space=pltpu.SMEM),
            pl.BlockSpec(memory_space=pltpu.HBM),
            pl.BlockSpec(memory_space=pltpu.HBM),
            pl.BlockSpec(memory_space=pltpu.HBM),
            pl.BlockSpec(memory_space=pltpu.HBM),
        ],
        out_specs=pl.BlockSpec(memory_space=pltpu.VMEM),
        scratch_shapes=[
            pltpu.VMEM(potential.shape, f32),
            pltpu.VMEM((atom_plane.shape[0] // 128, 128), jnp.int32),
            padded, padded, padded, whole, whole, whole,
            pltpu.VMEM((3,) + cells, f32),
            pltpu.VMEM((stored,) + cells, f32),
            pltpu.VMEM((stored, orbitals, cells_dev), jnp.bfloat16),
            pltpu.VMEM((stored, orbitals, cells_dev), jnp.bfloat16),
            pltpu.VMEM((2, 8, orbitals), f32),
            pltpu.VMEM((ranks, width_x, orbitals), f32),
            pltpu.VMEM((ranks, width_x, orbitals), f32),
            gram, gram, gram, gram, gram, gram, gram,
            dma((5,)),
            dma((3, 2)), dma((3, 2)), dma((3, 2)), dma((3, 2)),
            dma((nb, 2)), dma((nb, 2)),
            dma((ranks,)), dma((ranks,)), dma((ranks,)), dma((ranks,)),
            dma((2,)), dma((2,)),
            dma((2, CHUNKS)), dma((2, CHUNKS)), dma((2, CHUNKS)), dma((2, CHUNKS)),
            dma((2, CHUNKS)), dma((2, CHUNKS)),
        ],
        compiler_params=pltpu.CompilerParams(
            collective_id=0, has_side_effects=True, vmem_limit_bytes=60 * 1024 * 1024
        ),
        cost_estimate=pl.CostEstimate(
            flops=4 * cells_dev * orbitals * stored * orbitals,
            bytes_accessed=4 * orbitals * (3 * cells_dev + 2 * stored * orbitals),
            transcendentals=0,
        ),
    )(block_slot, filter_block, band_blocks, potential, atom_plane.reshape(-1, 128))
    shape = (1, stored, orbitals, orbitals)
    norm_factor = 1.0 / math.sqrt(cells_dev * ranks)
    return (products[0] * norm_factor).reshape(shape), (products[1] * norm_factor).reshape(shape)


def solution(mesh):
    return jax.shard_map(
        functools.partial(shards, mesh.shape["grid"], mesh.shape["band"]),
        mesh=mesh,
        in_specs=(
            P(("groups", "band"), "grid", "sub", None, None),
            P(("groups", "band"), None, "grid", "sub", None, None),
            P(("groups", "grid"), "sub", None),
            P("groups"),
            P("groups"),
        ),
        out_specs=(
            P(("groups", "band"), None, None, None),
            P(("groups", "band"), None, None, None),
        ),
        check_vma=False,
    )
```
